32 devices in a mesh: shot: 2 (over core), space: 16 (over z, y, x).
Axes of the slice: x: 2, y: 2, z: 4, core: 2. Of those that a mesh axis runs over, the one named last changes fastest.
Arguments:
- medium_celerity: float32 [32, 32, 512], P('space'), may hold values from 1400 to 3000
- preceding_wave_snapshot: bfloat16 [4, 32, 32, 512], P('shot', 'space'), may hold values from -0.5 to 1.5
- entry_wave_snapshot: bfloat16 [4, 32, 32, 512], P('shot', 'space'), may hold values from -0.5 to 1.5
- costate_beyond_snapshot: bfloat16 [4, 32, 32, 512], P('shot', 'space'), may hold values from -6 to 6
- costate_terminal_snapshot: bfloat16 [4, 32, 32, 512], P('shot', 'space'), may hold values from -6 to 6
- signature_series: float32 [6], replicated, may hold values from -8 to 8
- emitter_indicator: int32 [4, 1024], P('shot'), may hold values 0 or 1
- probe_locations: int32 [3, 1024], replicated, may hold values from 0 to 511, as said below
- acquired_recordings: float32 [4, 6, 1024], P('shot'), may hold values from 0 to 2
Outputs:
- final_field: bfloat16 [4, 32, 32, 512], P('shot', 'space')
- amplitude: float32 [4], P('shot')
- gradient: float32 [32, 32, 512], P('space')
The draws below stay inside these ranges and needn't reach their ends.
Inputs may be any that keep to these rules, and one draw needn't show every extreme that they name: probe_locations[0] is below 32, probe_locations[1] below 32, probe_locations[2] below 512; transducers may share a cell.
All inputs are finite; a program needn't handle non-finite values. No bound on the sum of `emitter_indicator` on one device may be relied on, other than what follows from the above.
Results may differ from the reference program's by a relative error of at most 0.033.
Values may be sent and summed in bfloat16 or wider, within the bound.
A program may use at most 576 MiB of HBM per device.

```python
import jax
import jax.numpy as jnp

ROWWISE_EXTENT = 32
LATERAL_EXTENT = 512
ELEMENT_TALLY = 1024
TICK_TALLY = 6
EMISSION_TALLY = 4
AXIAL_EXTENT = 32


def draw_probe_locations(key, part):
    first_key, second_key, third_key = jax.random.split(key, 3)
    depth = jax.random.randint(first_key, (ELEMENT_TALLY,), 0, AXIAL_EXTENT)
    across = jax.random.randint(second_key, (ELEMENT_TALLY,), 0, ROWWISE_EXTENT)
    along = jax.random.randint(third_key, (ELEMENT_TALLY,), 0, LATERAL_EXTENT)
    depth = depth.at[0].set(AXIAL_EXTENT - 1).at[1].set(0)
    across = across.at[0].set(ROWWISE_EXTENT - 1).at[1].set(0)
    along = along.at[0].set(LATERAL_EXTENT - 1).at[1].set(0)
    return jnp.stack([depth, across, along]).astype(jnp.int32)


def place_ends(drawn, key, low, top_value):
    place = [jax.random.randint(jax.random.fold_in(key, axis), (), 0, length) for axis, length in enumerate(drawn.shape)]
    main_axis = drawn.shape.index(max(drawn.shape))
    beside = place[:main_axis] + [(place[main_axis] + 1) % drawn.shape[main_axis]] + place[main_axis + 1:]
    return drawn.at[tuple(place)].set(low).at[tuple(beside)].set(top_value)


def block_levels(own_key, dims, cuts, smallest, largest):
    def one(dim, shards_of):
        draws = jax.random.uniform(jax.random.fold_in(jax.random.fold_in(own_key, 6), dim), (shards_of,), jnp.float32, smallest / len(cuts), largest / len(cuts))
        return jnp.repeat(jnp.exp(draws), dims[dim] // shards_of).reshape((-1,) + (1,) * (len(dims) - dim - 1))

    loudness = one(*cuts[0])
    for cut in cuts[1:]:
        loudness = loudness * one(*cut)
    return loudness


def normal_values(key, extent, spread, most, cuts=(), held_as=jnp.bfloat16):
    result = spread * jax.random.normal(key, extent, jnp.float32)
    if cuts:
        result = result * block_levels(key, extent, cuts, -0.22, 0.18)
    return jnp.clip(result, -most, most).astype(held_as)


def setup_inputs(seed: int = 0) -> dict:
    keys = jax.random.split(jax.random.key(seed), 10)
    return {
        "medium_celerity": jnp.clip(1400.0 + 1600.0 * jax.random.uniform(keys[0], (AXIAL_EXTENT, ROWWISE_EXTENT, LATERAL_EXTENT), jnp.float32) ** block_levels(keys[0], (AXIAL_EXTENT, ROWWISE_EXTENT, LATERAL_EXTENT), ((0, 16),), -0.2, 0.2), 1400.0, 3000.0),
        "preceding_wave_snapshot": jnp.clip(-0.5 + 2.0 * jax.random.uniform(keys[1], (EMISSION_TALLY, AXIAL_EXTENT, ROWWISE_EXTENT, LATERAL_EXTENT), jnp.float32) ** block_levels(keys[1], (EMISSION_TALLY, AXIAL_EXTENT, ROWWISE_EXTENT, LATERAL_EXTENT), ((0, 2), (1, 16)), -0.2, 0.2), -0.5, 1.5).astype(jnp.bfloat16),
        "entry_wave_snapshot": jnp.clip(-0.5 + 2.0 * jax.random.uniform(keys[2], (EMISSION_TALLY, AXIAL_EXTENT, ROWWISE_EXTENT, LATERAL_EXTENT), jnp.float32) ** block_levels(keys[2], (EMISSION_TALLY, AXIAL_EXTENT, ROWWISE_EXTENT, LATERAL_EXTENT), ((0, 2), (1, 16)), -0.2, 0.2), -0.5, 1.5).astype(jnp.bfloat16),
        "costate_beyond_snapshot": normal_values(keys[3], (EMISSION_TALLY, AXIAL_EXTENT, ROWWISE_EXTENT, LATERAL_EXTENT), 1.0, 6.0, ((0, 2), (1, 16))),
        "costate_terminal_snapshot": normal_values(keys[4], (EMISSION_TALLY, AXIAL_EXTENT, ROWWISE_EXTENT, LATERAL_EXTENT), 1.0, 6.0, ((0, 2), (1, 16))),
        "signature_series": normal_values(keys[5], (TICK_TALLY,), 2.0, 8.0, (), jnp.float32),
        "emitter_indicator": place_ends((jax.random.randint(keys[6], (EMISSION_TALLY, ELEMENT_TALLY), 0, 4) < 1).astype(jnp.int32), jax.random.fold_in(keys[6], 1), 0, 1),
        "probe_locations": draw_probe_locations(jax.random.fold_in(keys[9], 71), 0),
        "acquired_recordings": jnp.clip(2.0 * jax.random.uniform(keys[8], (EMISSION_TALLY, TICK_TALLY, ELEMENT_TALLY), jnp.float32) ** block_levels(keys[8], (EMISSION_TALLY, TICK_TALLY, ELEMENT_TALLY), ((0, 2),), -0.2, 0.2), 0.0, 2.0),
    }


SPEED_SCALE = 1.0 / 6000.0
EPSILON = 1e-6


def laplace(field):
    padded = jnp.pad(field, ((0, 0), (1, 1), (1, 1), (1, 1)))
    return (padded[:, 2:, 1:-1, 1:-1] + padded[:, :-2, 1:-1, 1:-1] + padded[:, 1:-1, 2:, 1:-1] + padded[:, 1:-1, :-2, 1:-1] + padded[:, 1:-1, 1:-1, 2:] + padded[:, 1:-1, 1:-1, :-2]) - 6.0 * field


def advance(earlier, current, courant, values, flat_index):
    current_f = current.astype(jnp.float32)
    following = 2.0 * current_f - earlier.astype(jnp.float32) + courant * laplace(current_f)
    shape = following.shape
    following = following.reshape(shape[0], -1).at[:, flat_index].add(values).reshape(shape)
    return following.astype(jnp.bfloat16)


def one_shot(courant, preceding_wave_snapshot, entry_wave_snapshot, costate_beyond_snapshot, costate_terminal_snapshot, signature_series, fire_row, flat_index, observed_row):
    history = [preceding_wave_snapshot, entry_wave_snapshot]
    traces = []
    for step_index in range(TICK_TALLY):
        following = advance(history[-2], history[-1], courant, fire_row * signature_series[step_index], flat_index)
        history.append(following)
        traces.append(following.reshape(1, -1)[:, flat_index].astype(jnp.float32))
    synthetic = jnp.stack(traces, axis=1)
    amplitude = jnp.sum(observed_row * synthetic, axis=(1, 2)) / (jnp.sum(synthetic * synthetic, axis=(1, 2)) + EPSILON)
    misfit = amplitude[:, None, None] * synthetic - observed_row
    later_field, now_field = costate_beyond_snapshot, costate_terminal_snapshot
    total = jnp.zeros((AXIAL_EXTENT, ROWWISE_EXTENT, LATERAL_EXTENT), jnp.float32)
    for step_index in range(TICK_TALLY, 0, -1):
        earlier_field = advance(later_field, now_field, courant, misfit[:, step_index - 1, :], flat_index)
        moment = step_index - 1
        curvature = history[moment + 2].astype(jnp.float32) - 2.0 * history[moment + 1].astype(jnp.float32) + history[moment].astype(jnp.float32)
        total = total + jnp.sum(earlier_field.astype(jnp.float32) * curvature, axis=0)
        later_field, now_field = now_field, earlier_field
    return history[-1], amplitude, total


def reference(medium_celerity, preceding_wave_snapshot, entry_wave_snapshot, costate_beyond_snapshot, costate_terminal_snapshot, signature_series, emitter_indicator, probe_locations, acquired_recordings):
    courant = (medium_celerity * SPEED_SCALE) ** 2
    flat_index = ((probe_locations[0] * ROWWISE_EXTENT + probe_locations[1]) * LATERAL_EXTENT + probe_locations[2]).astype(jnp.int32)
    inject_signal = emitter_indicator.astype(jnp.float32)
    finals = []
    amplitudes = []
    total = jnp.zeros((AXIAL_EXTENT, ROWWISE_EXTENT, LATERAL_EXTENT), jnp.float32)
    for experiment_ordinal in range(EMISSION_TALLY):
        lo_end = experiment_ordinal
        hi_end = experiment_ordinal + 1
        final_one, amplitude_one, total_one = one_shot(courant, preceding_wave_snapshot[lo_end:hi_end], entry_wave_snapshot[lo_end:hi_end], costate_beyond_snapshot[lo_end:hi_end], costate_terminal_snapshot[lo_end:hi_end], signature_series, inject_signal[lo_end:hi_end], flat_index, acquired_recordings[lo_end:hi_end])
        finals.append(final_one)
        amplitudes.append(amplitude_one)
        total = total + total_one
    weight = 2.0 * (1500.0 / medium_celerity) ** 3
    return jnp.concatenate(finals, axis=0), jnp.concatenate(amplitudes, axis=0), weight * total
```

```python
import functools

import jax
import jax.numpy as jnp
from jax import lax
from jax.experimental import pallas as pl
from jax.experimental.pallas import tpu as pltpu
from jax.sharding import PartitionSpec as P

SPEED_SCALE = 1.0 / 6000.0
EPSILON = 1e-06
MESH = pl.DeviceIdType.MESH
F32 = jnp.float32
BF16 = jnp.bfloat16


def kernel(
    peers,
    velocity,
    preceding,
    entry,
    beyond,
    terminal,
    signature,
    emitters,
    locations,
    recordings,
    final,
    amplitude,
    gradient,
    forward,
    backward,
    forward_halo,
    backward_halo,
    courant,
    partial,
    column_hot,
    tally,
    fired,
    recorded,
    sums,
    products,
    gathered,
    total,
    outgoing,
    incoming,
    forward_sent,
    forward_got,
    backward_sent,
    backward_got,
    sums_sent,
    sums_got,
    total_sent,
    total_got,
):
    me = lax.axis_index("space")
    core = lax.axis_index("shot")
    shots, planes, rows, cols = entry.shape
    ticks = recordings.shape[1]
    last = planes - 1
    shot_range, plane_range = range(shots), range(planes)

    barrier = pltpu.get_barrier_semaphore()
    for d in range(1, peers):
        pl.semaphore_signal(
            barrier, inc=1, device_id={"space": lax.rem(me + d, peers)}, device_id_type=MESH
        )
    pl.semaphore_signal(barrier, inc=1, device_id={"shot": 1 - core}, device_id_type=MESH)
    pl.semaphore_wait(barrier, peers)

    def hop(field, halo, sent, got, side, j):
        return pltpu.make_async_remote_copy(
            src_ref=field.at[:, last if side == 0 else 0],
            dst_ref=halo.at[side, j],
            send_sem=sent.at[side, j],
            recv_sem=got.at[side, j],
            device_id={"space": me + 1 if side == 0 else me - 1},
            device_id_type=MESH,
        )

    def has_target(side):
        return me < peers - 1 if side == 0 else me > 0

    def has_source(side):
        return me > 0 if side == 0 else me < peers - 1

    def send(side, *args):
        @pl.when(has_target(side))
        def _():
            hop(*args[:4], side, args[4]).start()

    def receive(side, *args):
        @pl.when(has_source(side))
        def _():
            hop(*args[:4], side, args[4]).wait_recv()

    def drain(side, *args):
        @pl.when(has_target(side))
        def _():
            hop(*args[:4], side, args[4]).wait_send()

    ahead = [preceding, entry] + [forward.at[j] for j in range(ticks - 1)] + [final]
    back = [beyond, terminal] + [backward.at[j] for j in range(ticks)]
    ahead_link = (forward_halo, forward_sent, forward_got)
    back_link = (backward_halo, backward_sent, backward_got)

    for side in (1, 0):
        send(side, entry, *ahead_link, 0)
    for side in (1, 0):
        send(side, terminal, *back_link, 0)

    for side, here in ((0, me == 0), (1, me == peers - 1)):

        @pl.when(here)
        def _(side=side):
            forward_halo[side] = jnp.zeros_like(forward_halo[side])
            backward_halo[side] = jnp.zeros_like(backward_halo[side])

    courant[...] = (velocity[...] * SPEED_SCALE) ** 2

    probes = locations.shape[1]
    row_of = (locations[0:1, :] - me * planes) * rows + locations[1:2, :]
    row_hot = lax.broadcasted_iota(jnp.int32, (planes * rows, probes), 0) == row_of
    column_hot[...] = jnp.where(
        lax.broadcasted_iota(jnp.int32, (cols, probes), 0) == locations[2:3, :], 1.0, 0.0
    ).astype(BF16)

    def spread(left):
        return lax.dot_general(
            left, column_hot[...], (((1,), (1,)), ((), ())), preferred_element_type=F32
        )

    cells = planes * rows
    firing = emitters[...].astype(F32)
    lefts = [jnp.where(row_hot, 1.0, 0.0)]
    lefts += [jnp.where(row_hot, firing[s : s + 1], 0.0) for s in shot_range]
    placed = spread(jnp.concatenate(lefts, axis=0).astype(BF16))
    tally[...] = placed[:cells].reshape(planes, rows, cols)
    fired[...] = placed[cells:].reshape(shots, planes, rows, cols)

    def record(k):
        lefts = []
        for s in shot_range:
            row = recordings[s, k : k + 1, :]
            high = row.astype(BF16).astype(F32)
            lefts.append(jnp.where(row_hot, high, 0.0).astype(BF16))
            lefts.append(jnp.where(row_hot, row - high, 0.0).astype(BF16))
        both = spread(jnp.concatenate(lefts, axis=0)).reshape(shots, 2, planes, rows, cols)
        recorded[k] = both[:, 0] + both[:, 1]

    row_at = lax.broadcasted_iota(jnp.int32, (rows, cols), 0)
    col_at = lax.broadcasted_iota(jnp.int32, (rows, cols), 1)

    def inner(earlier, current, s, z):
        x = current[s, z].astype(F32)
        around = jnp.where(row_at == rows - 1, 0.0, pltpu.roll(x, rows - 1, 0))
        around += jnp.where(row_at == 0, 0.0, pltpu.roll(x, 1, 0))
        around += jnp.where(col_at == cols - 1, 0.0, pltpu.roll(x, cols - 1, 1))
        around += jnp.where(col_at == 0, 0.0, pltpu.roll(x, 1, 1))
        if z < last:
            around += current[s, z + 1].astype(F32)
        if z > 0:
            around += current[s, z - 1].astype(F32)
        return 2.0 * x - earlier[s, z].astype(F32) + courant[z] * (around - 6.0 * x)

    order = [0] + ([last] if last else []) + list(range(1, last))

    def finish(fields, link, j, moving):
        following = fields[j + 2]
        for z in order:
            if z == 0:
                receive(0, fields[j + 1], *link, j)
            if z == last:
                receive(1, fields[j + 1], *link, j)
            for s in shot_range:
                value = partial[s, z]
                if z == 0:
                    value += courant[z] * link[0][0, j, s].astype(F32)
                if z == last:
                    value += courant[z] * link[0][1, j, s].astype(F32)
                following[s, z] = value.astype(BF16)
            if moving and z == 0:
                send(1, following, *link, j + 1)
            if moving and z == last:
                send(0, following, *link, j + 1)

    def start_forward(j):
        for s in shot_range:
            for z in plane_range:
                partial[s, z] = (
                    inner(ahead[j], ahead[j + 1], s, z) + signature[j] * fired[s, z]
                )

    def correlate(k):
        for s in shot_range:
            top, bottom = 0.0, 0.0
            for z in plane_range:
                p = ahead[k + 2][s, z].astype(F32)
                top += p * recorded[k, s, z]
                bottom += p * p * tally[z]
            if k:
                top += products[s, 0]
                bottom += products[s, 1]
            products[s, 0] = top
            products[s, 1] = bottom

    start_forward(0)
    for j in range(ticks):
        finish(ahead, ahead_link, j, j < ticks - 1)
        if j < ticks - 1:
            start_forward(j + 1)
            record(j)
            correlate(j)
            if j == ticks - 2:
                record(ticks - 1)
        else:
            correlate(j)

    line = lax.broadcasted_iota(jnp.int32, (8, 128), 0)
    block = jnp.zeros((8, 128), F32)
    for s in shot_range:
        block = jnp.where(line == 2 * s, jnp.sum(products[s, 0]), block)
        block = jnp.where(line == 2 * s + 1, jnp.sum(products[s, 1]), block)
    sums[...] = block

    def share(d):
        return pltpu.make_async_remote_copy(
            src_ref=sums,
            dst_ref=gathered.at[me],
            send_sem=sums_sent.at[d],
            recv_sem=sums_got.at[me],
            device_id={"space": lax.rem(me + d, peers)},
            device_id_type=MESH,
        )

    def shared(d):
        other = lax.rem(me + d, peers)
        return pltpu.make_async_remote_copy(
            src_ref=sums,
            dst_ref=gathered.at[other],
            send_sem=sums_sent.at[d],
            recv_sem=sums_got.at[other],
            device_id={"space": other},
            device_id_type=MESH,
        )

    for d in range(1, peers):
        share(d).start()
    gathered[me] = block

    for s in shot_range:
        for z in plane_range:
            partial[s, z] = inner(beyond, terminal, s, z) - recorded[ticks - 1, s, z]

    for d in range(1, peers):
        shared(d).wait_recv()
    whole = gathered[0]
    for i in range(1, peers):
        whole += gathered[i]
    scales = []
    for s in shot_range:
        scale = whole[2 * s : 2 * s + 1] / (whole[2 * s + 1 : 2 * s + 2] + EPSILON)
        scales.append(scale[:, :1])
        amplitude[s] = jnp.max(scale)

    for s in shot_range:
        for z in plane_range:
            p = final[s, z].astype(F32)
            partial[s, z] = partial[s, z] + scales[s] * (tally[z] * p)

    def gather_total(j, z):
        moment = ticks - 1 - j
        value = 0.0
        for s in shot_range:
            curvature = (
                ahead[moment + 2][s, z].astype(F32)
                - 2.0 * ahead[moment + 1][s, z].astype(F32)
                + ahead[moment][s, z].astype(F32)
            )
            value += back[j + 2][s, z].astype(F32) * curvature
        return value if j == 0 else total[z] + value

    def swap(z):
        return pltpu.make_async_remote_copy(
            src_ref=outgoing.at[z],
            dst_ref=incoming.at[z],
            send_sem=total_sent.at[z],
            recv_sem=total_got.at[z],
            device_id={"shot": 1 - core},
            device_id_type=MESH,
        )

    for j in range(ticks):
        finish(back, back_link, j, j < ticks - 1)
        if j < ticks - 1:
            k = ticks - 2 - j
            for s in shot_range:
                for z in plane_range:
                    source = scales[s] * (tally[z] * ahead[k + 2][s, z].astype(F32))
                    partial[s, z] = (
                        inner(back[j + 1], back[j + 2], s, z) + source - recorded[k, s, z]
                    )
            for z in plane_range:
                total[z] = gather_total(j, z)
        else:
            for z in plane_range:
                outgoing[z] = gather_total(j, z).astype(BF16)
                swap(z).start()

    weight = 2.0 * (1500.0 / velocity[...]) ** 3
    for z in plane_range:
        swap(z).wait_recv()
        gradient[z] = weight[z] * (outgoing[z].astype(F32) + incoming[z].astype(F32))

    for fields, link in ((ahead, ahead_link), (back, back_link)):
        for j in range(ticks):
            for side in (0, 1):
                drain(side, fields[j + 1], *link, j)
    for d in range(1, peers):
        share(d).wait_send()
    for z in plane_range:
        swap(z).wait_send()


def body(peers, *args):
    medium, entry, locations, recordings = args[0], args[2], args[7], args[8]
    shots, planes, rows, cols = entry.shape
    ticks = recordings.shape[1]
    probes = locations.shape[1]
    vmem = pl.BlockSpec(memory_space=pltpu.VMEM)
    smem = pl.BlockSpec(memory_space=pltpu.SMEM)
    slab = (planes, rows, cols)
    dma = pltpu.SemaphoreType.DMA
    return pl.pallas_call(
        functools.partial(kernel, peers),
        out_shape=(
            jax.ShapeDtypeStruct(entry.shape, BF16),
            jax.ShapeDtypeStruct((shots,), F32),
            jax.ShapeDtypeStruct(medium.shape, F32),
        ),
        in_specs=[vmem] * 5 + [smem] + [vmem] * 3,
        out_specs=(vmem, smem, vmem),
        scratch_shapes=[
            pltpu.VMEM((ticks - 1, shots) + slab, BF16),
            pltpu.VMEM((ticks, shots) + slab, BF16),
            pltpu.VMEM((2, ticks, shots, rows, cols), BF16),
            pltpu.VMEM((2, ticks, shots, rows, cols), BF16),
            pltpu.VMEM(slab, F32),
            pltpu.VMEM((shots,) + slab, F32),
            pltpu.VMEM((cols, probes), BF16),
            pltpu.VMEM(slab, F32),
            pltpu.VMEM((shots,) + slab, F32),
            pltpu.VMEM((ticks, shots) + slab, F32),
            pltpu.VMEM((8, 128), F32),
            pltpu.VMEM((shots, 2, rows, cols), F32),
            pltpu.VMEM((peers, 8, 128), F32),
            pltpu.VMEM(slab, F32),
            pltpu.VMEM(slab, BF16),
            pltpu.VMEM(slab, BF16),
            dma((2, ticks)),
            dma((2, ticks)),
            dma((2, ticks)),
            dma((2, ticks)),
            dma((peers,)),
            dma((peers,)),
            dma((planes,)),
            dma((planes,)),
        ],
        compiler_params=pltpu.CompilerParams(
            collective_id=0, has_side_effects=True, vmem_limit_bytes=40 * 1024 * 1024
        ),
    )(*args)


def solution(mesh):
    placed = (
        P("space", None, None),
        P("shot", "space", None, None),
        P("shot", "space", None, None),
        P("shot", "space", None, None),
        P("shot", "space", None, None),
        P(),
        P("shot", None),
        P(),
        P("shot", None, None),
    )
    return jax.shard_map(
        functools.partial(body, mesh.shape["space"]),
        mesh=mesh,
        in_specs=placed,
        out_specs=(P("shot", "space", None, None), P("shot"), P("space", None, None)),
        check_vma=False,
    )
```

```python
import functools

import jax
import jax.numpy as jnp
from jax import lax
from jax.experimental import pallas as pl
from jax.experimental.pallas import tpu as pltpu
from jax.sharding import PartitionSpec as P

SPEED_SCALE = 1.0 / 6000.0
EPSILON = 1e-06
MESH = pl.DeviceIdType.MESH
F32 = jnp.float32
BF16 = jnp.bfloat16


def kernel(
    peers,
    velocity_in,
    preceding_in,
    entry_in,
    beyond_in,
    terminal_in,
    signature,
    emitters,
    locations,
    recordings,
    final,
    amplitude,
    gradient,
    velocity,
    preceding,
    entry,
    beyond,
    terminal,
    forward,
    backward,
    forward_halo,
    backward_halo,
    forward_ring,
    backward_ring,
    preceding_ring,
    beyond_ring,
    final_ring,
    velocity_ring,
    courant,
    courant_ring,
    partial,
    column_hot,
    tally,
    fired,
    recorded,
    sums,
    products,
    gathered,
    total,
    outgoing,
    incoming,
    loaded,
    forward_sent,
    forward_got,
    backward_sent,
    backward_got,
    preceding_sent,
    preceding_got,
    beyond_sent,
    beyond_got,
    final_sent,
    final_got,
    velocity_sent,
    velocity_got,
    sums_sent,
    sums_got,
    total_sent,
    total_got,
):
    me = lax.axis_index("space")
    core = lax.axis_index("shot")
    shots, planes, rows, cols = entry.shape
    ticks = recordings.shape[1]
    last = planes - 1
    shot_range, plane_range, sides = range(shots), range(planes), (0, 1)
    pairs = ticks // 2

    barrier = pltpu.get_barrier_semaphore()
    for d in range(1, peers):
        pl.semaphore_signal(
            barrier, inc=1, device_id={"space": lax.rem(me + d, peers)}, device_id_type=MESH
        )
    pl.semaphore_signal(barrier, inc=1, device_id={"shot": 1 - core}, device_id_type=MESH)

    loads = [
        pltpu.make_async_copy(source, target, loaded.at[i])
        for i, (source, target) in enumerate(
            (
                (velocity_in, velocity),
                (preceding_in, preceding),
                (entry_in, entry),
                (beyond_in, beyond),
                (terminal_in, terminal),
            )
        )
    ]
    for load in loads:
        load.start()

    pl.semaphore_wait(barrier, peers)

    def hop(side, source, target, sent, got):
        return pltpu.make_async_remote_copy(
            src_ref=source,
            dst_ref=target,
            send_sem=sent,
            recv_sem=got,
            device_id={"space": me + 1 if side == 0 else me - 1},
            device_id_type=MESH,
        )

    started = []

    def send(side, *args):
        @pl.when(me < peers - 1 if side == 0 else me > 0)
        def _():
            hop(side, *args).start()

        started.append((side, args))

    def receive(side, *args):
        @pl.when(me > 0 if side == 0 else me < peers - 1)
        def _():
            hop(side, *args).wait_recv()

    def pair_args(side, field, link, e, s):
        halo, sent, got = link
        low = planes - 2 if side == 0 else 0
        return (
            field.at[s, pl.ds(low, 2)],
            halo.at[side, e, s],
            sent.at[side, e, s],
            got.at[side, e, s],
        )

    def plane_args(side, field, ring, sent, got, s):
        edge = last if side == 0 else 0
        return field.at[s, edge], ring.at[side, s], sent.at[side, s], got.at[side, s]

    def velocity_args(side):
        edge = last if side == 0 else 0
        return (
            velocity_in.at[edge],
            velocity_ring.at[side],
            velocity_sent.at[side],
            velocity_got.at[side],
        )

    ahead = [preceding, entry] + [forward.at[j] for j in range(ticks - 1)] + [final]
    back = [beyond, terminal] + [backward.at[j] for j in range(ticks)]
    ahead_link = (forward_halo, forward_sent, forward_got)
    back_link = (backward_halo, backward_sent, backward_got)
    preceding_link = (preceding_ring, preceding_sent, preceding_got)
    beyond_link = (beyond_ring, beyond_sent, beyond_got)
    final_link = (final_ring, final_sent, final_got)

    for s in shot_range:
        for side in sides:
            send(side, *pair_args(side, entry_in, ahead_link, 0, s))
        for side in sides:
            send(side, *plane_args(side, preceding_in, *preceding_link, s))
        if s == 0:
            for side in sides:
                send(side, *velocity_args(side))
    for s in shot_range:
        for side in sides:
            send(side, *pair_args(side, terminal_in, back_link, 0, s))
        for side in sides:
            send(side, *plane_args(side, beyond_in, *beyond_link, s))

    for side, here in ((0, me == 0), (1, me == peers - 1)):

        @pl.when(here)
        def _(side=side):
            for ring in (
                forward_halo,
                backward_halo,
                preceding_ring,
                beyond_ring,
                final_ring,
                velocity_ring,
            ):
                ring[side] = jnp.zeros_like(ring[side])

    probes = locations.shape[1]
    wide = planes + 2
    cells = wide * rows
    row_of = (locations[0:1, :] - me * planes + 1) * rows + locations[1:2, :]
    row_hot = lax.broadcasted_iota(jnp.int32, (cells, probes), 0) == row_of
    column_hot[...] = jnp.where(
        lax.broadcasted_iota(jnp.int32, (cols, probes), 0) == locations[2:3, :], 1.0, 0.0
    ).astype(BF16)

    def spread(left):
        return lax.dot_general(
            left, column_hot[...], (((1,), (1,)), ((), ())), preferred_element_type=F32
        )

    firing = emitters[...].astype(F32)
    lefts = [jnp.where(row_hot, 1.0, 0.0)]
    lefts += [jnp.where(row_hot, firing[s : s + 1], 0.0) for s in shot_range]
    placed = spread(jnp.concatenate(lefts, axis=0).astype(BF16))
    tally[...] = placed[:cells].reshape(wide, rows, cols)
    fired[...] = placed[cells:].reshape(shots, wide, rows, cols)

    def record(k):
        for s in shot_range:
            row = recordings[s, k : k + 1, :]
            high = row.astype(BF16).astype(F32)
            lefts = [
                jnp.where(row_hot, high, 0.0).astype(BF16),
                jnp.where(row_hot, row - high, 0.0).astype(BF16),
            ]
            both = spread(jnp.concatenate(lefts, axis=0)).reshape(2, wide, rows, cols)
            recorded[k, s] = both[0] + both[1]

    row_at = lax.broadcasted_iota(jnp.int32, (rows, cols), 0)
    col_at = lax.broadcasted_iota(jnp.int32, (rows, cols), 1)

    def in_plane(x):
        around = jnp.where(row_at == rows - 1, 0.0, pltpu.roll(x, rows - 1, 0))
        around += jnp.where(row_at == 0, 0.0, pltpu.roll(x, 1, 0))
        around += jnp.where(col_at == cols - 1, 0.0, pltpu.roll(x, cols - 1, 1))
        around += jnp.where(col_at == 0, 0.0, pltpu.roll(x, 1, 1))
        return around

    def inner(earlier, current, s, z):
        x = current[s, z].astype(F32)
        around = in_plane(x)
        if z < last:
            around += current[s, z + 1].astype(F32)
        if z > 0:
            around += current[s, z - 1].astype(F32)
        return 2.0 * x - earlier[s, z].astype(F32) + courant[z] * (around - 6.0 * x)

    def near(halo, side, e, s):
        return halo[side, e, s, 1 - side]

    def begin(fields, e, s, source):
        for z in plane_range:
            partial[s, z] = inner(fields[2 * e], fields[2 * e + 1], s, z) + source(
                2 * e, s, z + 1, fields
            )

    def two_steps(fields, link, rings, e, s, before, source, ring_source):
        halo = link[0]
        j = 2 * e
        earlier, current, middle, after = fields[j : j + 4]
        for z in plane_range:
            value = partial[s, z]
            if z == 0:
                value += courant[z] * near(halo, 0, e, s).astype(F32)
            if z == last:
                value += courant[z] * near(halo, 1, e, s).astype(F32)
            middle[s, z] = value.astype(BF16)
        for side in sides:
            x = near(halo, side, e, s).astype(F32)
            around = in_plane(x) + halo[side, e, s, side].astype(F32)
            around += current[s, 0 if side == 0 else last].astype(F32)
            old = before[side, s] if e == 0 else rings[side, e - 1, s]
            value = 2.0 * x - old.astype(F32) + courant_ring[side] * (around - 6.0 * x)
            rings[side, e, s] = (value + ring_source(e, s, side)).astype(BF16)
        for z in plane_range:
            value = inner(current, middle, s, z) + source(j + 1, s, z + 1, fields)
            if z == 0:
                value += courant[z] * rings[0, e, s].astype(F32)
            if z == last:
                value += courant[z] * rings[1, e, s].astype(F32)
            after[s, z] = value.astype(BF16)
        if e < pairs - 1:
            for side in sides:
                send(side, *pair_args(side, after, link, e + 1, s))

    def fire(j, s, w, fields):
        return signature[j] * fired[s, w]

    def fire_ring(e, s, side):
        return signature[2 * e] * fired[s, 0 if side == 0 else wide - 1]

    def correlate(k, s):
        top, bottom = 0.0, 0.0
        for z in plane_range:
            p = ahead[k + 2][s, z].astype(F32)
            top += p * recorded[k, s, z + 1]
            bottom += p * p * tally[z + 1]
        if k:
            top += products[s, 0]
            bottom += products[s, 1]
        products[s, 0] = top
        products[s, 1] = bottom

    for load in loads:
        load.wait()
    courant[...] = (velocity[...] * SPEED_SCALE) ** 2
    for s in shot_range:
        begin(ahead, 0, s, fire)
    for k in range(ticks):
        record(k)
    for side in sides:
        receive(side, *velocity_args(side))
    courant_ring[...] = (velocity_ring[...] * SPEED_SCALE) ** 2

    for e in range(pairs):
        for s in shot_range:
            for side in sides:
                receive(side, *pair_args(side, ahead[2 * e + 1], ahead_link, e, s))
            if e == 0:
                for side in sides:
                    receive(side, *plane_args(side, preceding_in, *preceding_link, s))
            two_steps(
                ahead, ahead_link, forward_ring, e, s, preceding_ring, fire, fire_ring
            )
            if e < pairs - 1:
                begin(ahead, e + 1, s, fire)
            else:
                for side in sides:
                    send(side, *plane_args(side, final, *final_link, s))
            correlate(2 * e, s)
            correlate(2 * e + 1, s)

    line = lax.broadcasted_iota(jnp.int32, (8, 128), 0)
    block = jnp.zeros((8, 128), F32)
    for s in shot_range:
        block = jnp.where(line == 2 * s, jnp.sum(products[s, 0]), block)
        block = jnp.where(line == 2 * s + 1, jnp.sum(products[s, 1]), block)
    sums[...] = block

    def share(d):
        return pltpu.make_async_remote_copy(
            src_ref=sums,
            dst_ref=gathered.at[me],
            send_sem=sums_sent.at[d],
            recv_sem=sums_got.at[me],
            device_id={"space": lax.rem(me + d, peers)},
            device_id_type=MESH,
        )

    def shared(d):
        other = lax.rem(me + d, peers)
        return pltpu.make_async_remote_copy(
            src_ref=sums,
            dst_ref=gathered.at[other],
            send_sem=sums_sent.at[d],
            recv_sem=sums_got.at[other],
            device_id={"space": other},
            device_id_type=MESH,
        )

    for d in range(1, peers):
        share(d).start()
    gathered[me] = block

    for s in shot_range:
        begin(back, 0, s, lambda j, s, w, fields: -recorded[ticks - 1, s, w])
        for side in sides:
            receive(side, *pair_args(side, terminal_in, back_link, 0, s))
            receive(side, *plane_args(side, beyond_in, *beyond_link, s))
            receive(side, *plane_args(side, final, *final_link, s))

    for d in range(1, peers):
        shared(d).wait_recv()
    whole = gathered[0]
    for i in range(1, peers):
        whole += gathered[i]
    scales = []
    for s in shot_range:
        scale = whole[2 * s : 2 * s + 1] / (whole[2 * s + 1 : 2 * s + 2] + EPSILON)
        scales.append(scale[:, :1])
        amplitude[s] = jnp.max(scale)

    for s in shot_range:
        for z in plane_range:
            p = final[s, z].astype(F32)
            partial[s, z] = partial[s, z] + scales[s] * (tally[z + 1] * p)

    def residue(j, s, w, fields):
        k = ticks - 1 - j
        p = ahead[k + 2][s, w - 1].astype(F32)
        return scales[s] * (tally[w] * p) - recorded[k, s, w]

    def residue_ring(e, s, side):
        w = 0 if side == 0 else wide - 1
        p = final_ring[side, s] if e == 0 else near(forward_halo, side, pairs - e, s)
        return scales[s] * (tally[w] * p.astype(F32)) - recorded[ticks - 1 - 2 * e, s, w]

    def gather_total(j, z):
        moment = ticks - 1 - j
        value = 0.0
        for s in shot_range:
            curvature = (
                ahead[moment + 2][s, z].astype(F32)
                - 2.0 * ahead[moment + 1][s, z].astype(F32)
                + ahead[moment][s, z].astype(F32)
            )
            value += back[j + 2][s, z].astype(F32) * curvature
        return value if j == 0 else total[z] + value

    def swap(z):
        return pltpu.make_async_remote_copy(
            src_ref=outgoing.at[z],
            dst_ref=incoming.at[z],
            send_sem=total_sent.at[z],
            recv_sem=total_got.at[z],
            device_id={"shot": 1 - core},
            device_id_type=MESH,
        )

    for e in range(pairs):
        for s in shot_range:
            if e:
                for side in sides:
                    receive(side, *pair_args(side, back[2 * e + 1], back_link, e, s))
            two_steps(
                back, back_link, backward_ring, e, s, beyond_ring, residue, residue_ring
            )
            if e < pairs - 1:
                begin(back, e + 1, s, residue)
        for z in plane_range:
            total[z] = gather_total(2 * e, z)
            value = gather_total(2 * e + 1, z)
            if e < pairs - 1:
                total[z] = value
            else:
                outgoing[z] = value.astype(BF16)
                swap(z).start()

    for z in plane_range:
        weight = 2.0 * (1500.0 / velocity[z]) ** 3
        swap(z).wait_recv()
        gradient[z] = weight * (outgoing[z].astype(F32) + incoming[z].astype(F32))

    for side, args in started:

        @pl.when(me < peers - 1 if side == 0 else me > 0)
        def _(side=side, args=args):
            hop(side, *args).wait_send()

    for d in range(1, peers):
        share(d).wait_send()
    for z in plane_range:
        swap(z).wait_send()


def body(peers, *args):
    medium, entry, locations, recordings = args[0], args[2], args[7], args[8]
    shots, planes, rows, cols = entry.shape
    ticks = recordings.shape[1]
    probes = locations.shape[1]
    vmem = pl.BlockSpec(memory_space=pltpu.VMEM)
    smem = pl.BlockSpec(memory_space=pltpu.SMEM)
    slab = (planes, rows, cols)
    wide = (planes + 2, rows, cols)
    pairs = ticks // 2
    dma = pltpu.SemaphoreType.DMA
    return pl.pallas_call(
        functools.partial(kernel, peers),
        out_shape=(
            jax.ShapeDtypeStruct(entry.shape, BF16),
            jax.ShapeDtypeStruct((shots,), F32),
            jax.ShapeDtypeStruct(medium.shape, F32),
        ),
        in_specs=[pl.BlockSpec(memory_space=pl.ANY)] * 5 + [smem] + [vmem] * 3,
        out_specs=(vmem, smem, vmem),
        scratch_shapes=[
            pltpu.VMEM(slab, F32),
            pltpu.VMEM((shots,) + slab, BF16),
            pltpu.VMEM((shots,) + slab, BF16),
            pltpu.VMEM((shots,) + slab, BF16),
            pltpu.VMEM((shots,) + slab, BF16),
            pltpu.VMEM((ticks - 1, shots) + slab, BF16),
            pltpu.VMEM((ticks, shots) + slab, BF16),
            pltpu.VMEM((2, pairs, shots, 2, rows, cols), BF16),
            pltpu.VMEM((2, pairs, shots, 2, rows, cols), BF16),
            pltpu.VMEM((2, pairs, shots, rows, cols), BF16),
            pltpu.VMEM((2, pairs, shots, rows, cols), BF16),
            pltpu.VMEM((2, shots, rows, cols), BF16),
            pltpu.VMEM((2, shots, rows, cols), BF16),
            pltpu.VMEM((2, shots, rows, cols), BF16),
            pltpu.VMEM((2, rows, cols), F32),
            pltpu.VMEM(slab, F32),
            pltpu.VMEM((2, rows, cols), F32),
            pltpu.VMEM((shots,) + slab, F32),
            pltpu.VMEM((cols, probes), BF16),
            pltpu.VMEM(wide, F32),
            pltpu.VMEM((shots,) + wide, F32),
            pltpu.VMEM((ticks, shots) + wide, F32),
            pltpu.VMEM((8, 128), F32),
            pltpu.VMEM((shots, 2, rows, cols), F32),
            pltpu.VMEM((peers, 8, 128), F32),
            pltpu.VMEM(slab, F32),
            pltpu.VMEM(slab, BF16),
            pltpu.VMEM(slab, BF16),
            dma((5,)),
            dma((2, pairs, shots)),
            dma((2, pairs, shots)),
            dma((2, pairs, shots)),
            dma((2, pairs, shots)),
            dma((2, shots)),
            dma((2, shots)),
            dma((2, shots)),
            dma((2, shots)),
            dma((2, shots)),
            dma((2, shots)),
            dma((2,)),
            dma((2,)),
            dma((peers,)),
            dma((peers,)),
            dma((planes,)),
            dma((planes,)),
        ],
        compiler_params=pltpu.CompilerParams(
            collective_id=0, has_side_effects=True, vmem_limit_bytes=40 * 1024 * 1024
        ),
    )(*args)


def solution(mesh):
    placed = (
        P("space", None, None),
        P("shot", "space", None, None),
        P("shot", "space", None, None),
        P("shot", "space", None, None),
        P("shot", "space", None, None),
        P(),
        P("shot", None),
        P(),
        P("shot", None, None),
    )
    return jax.shard_map(
        functools.partial(body, mesh.shape["space"]),
        mesh=mesh,
        in_specs=placed,
        out_specs=(P("shot", "space", None, None), P("shot"), P("space", None, None)),
        check_vma=False,
    )
```

```python
import functools

import jax
import jax.numpy as jnp
from jax import lax
from jax.experimental import pallas as pl
from jax.experimental.pallas import tpu as pltpu
from jax.sharding import PartitionSpec as P

SPEED_SCALE = 1.0 / 6000.0
EPSILON = 1e-06
MESH = pl.DeviceIdType.MESH
F32 = jnp.float32
BF16 = jnp.bfloat16


def kernel(
    peers,
    velocity_in,
    preceding_in,
    entry_in,
    beyond_in,
    terminal_in,
    signature,
    emitters,
    locations,
    recordings,
    final,
    amplitude,
    gradient,
    velocity,
    preceding,
    entry,
    beyond,
    terminal,
    forward,
    backward,
    forward_halo,
    backward_halo,
    forward_ring,
    backward_ring,
    courant_edge,
    courant,
    courant_ring,
    partial,
    column_hot,
    tally,
    fired,
    recorded,
    sums,
    products,
    gathered,
    total,
    outgoing,
    incoming,
    loaded,
    forward_sent,
    forward_got,
    backward_sent,
    backward_got,
    courant_sent,
    courant_got,
    sums_sent,
    sums_got,
    total_sent,
    total_got,
):
    me = lax.axis_index("space")
    core = lax.axis_index("shot")
    shots, planes, rows, cols = entry.shape
    ticks = recordings.shape[1]
    last = planes - 1
    shot_range, plane_range, sides = range(shots), range(planes), (0, 1)
    pairs = ticks // 2

    barrier = pltpu.get_barrier_semaphore()
    for d in range(1, peers):
        pl.semaphore_signal(
            barrier, inc=1, device_id={"space": lax.rem(me + d, peers)}, device_id_type=MESH
        )
    pl.semaphore_signal(barrier, inc=1, device_id={"shot": 1 - core}, device_id_type=MESH)

    loads = [
        pltpu.make_async_copy(source, target, loaded.at[i])
        for i, (source, target) in enumerate(
            (
                (velocity_in, velocity),
                (preceding_in, preceding),
                (entry_in, entry),
                (beyond_in, beyond),
                (terminal_in, terminal),
            )
        )
    ]
    for load in loads:
        load.start()

    pl.semaphore_wait(barrier, peers)

    def hop(side, source, target, sent, got):
        return pltpu.make_async_remote_copy(
            src_ref=source,
            dst_ref=target,
            send_sem=sent,
            recv_sem=got,
            device_id={"space": me + 1 if side == 0 else me - 1},
            device_id_type=MESH,
        )

    started = []

    def send(side, *args):
        @pl.when(me < peers - 1 if side == 0 else me > 0)
        def _():
            hop(side, *args).start()

        started.append((side, args))

    def receive(side, *args):
        @pl.when(me > 0 if side == 0 else me < peers - 1)
        def _():
            hop(side, *args).wait_recv()

    def pair_args(side, field, link, e, s):
        halo, sent, got = link
        low = planes - 2 if side == 0 else 0
        return (
            field.at[s, pl.ds(low, 2)],
            halo.at[side, e, s],
            sent.at[side, e, s],
            got.at[side, e, s],
        )

    def plane_args(side, field, link, j, s):
        halo, sent, got = link
        edge, at = last if side == 0 else 0, j * pairs
        return (
            field.at[s, edge],
            halo.at[side, 0, s, j],
            sent.at[side, at, s],
            got.at[side, at, s],
        )

    def courant_args(side):
        return (
            courant_edge.at[side],
            courant_ring.at[side],
            courant_sent.at[side],
            courant_got.at[side],
        )

    ahead = [preceding, entry] + [forward.at[j] for j in range(ticks - 1)] + [final]
    back = [beyond, terminal] + [backward.at[j] for j in range(ticks)]
    ahead_link = (forward_halo, forward_sent, forward_got)
    back_link = (backward_halo, backward_sent, backward_got)

    for s in shot_range:
        for side in sides:
            send(side, *plane_args(side, entry_in, ahead_link, 0, s))

    for side, here in ((0, me == 0), (1, me == peers - 1)):

        @pl.when(here)
        def _(side=side):
            for ring in (
                forward_halo,
                backward_halo,
                courant_ring,
            ):
                ring[side] = jnp.zeros_like(ring[side])

    probes = locations.shape[1]
    wide = planes + 2
    cells = wide * rows
    row_of = (locations[0:1, :] - me * planes + 1) * rows + locations[1:2, :]
    row_hot = lax.broadcasted_iota(jnp.int32, (cells, probes), 0) == row_of
    column_hot[...] = jnp.where(
        lax.broadcasted_iota(jnp.int32, (cols, probes), 0) == locations[2:3, :], 1.0, 0.0
    ).astype(BF16)

    def spread(left):
        return lax.dot_general(
            left, column_hot[...], (((1,), (1,)), ((), ())), preferred_element_type=F32
        )

    firing = emitters[...].astype(F32)
    lefts = [jnp.where(row_hot, 1.0, 0.0)]
    lefts += [jnp.where(row_hot, firing[s : s + 1], 0.0) for s in shot_range]
    placed = spread(jnp.concatenate(lefts, axis=0).astype(BF16))
    tally[...] = placed[:cells].reshape(wide, rows, cols)
    fired[...] = placed[cells:].reshape(shots, wide, rows, cols)

    def record(k):
        for s in shot_range:
            row = recordings[s, k : k + 1, :]
            high = row.astype(BF16).astype(F32)
            lefts = [
                jnp.where(row_hot, high, 0.0).astype(BF16),
                jnp.where(row_hot, row - high, 0.0).astype(BF16),
            ]
            both = spread(jnp.concatenate(lefts, axis=0)).reshape(2, wide, rows, cols)
            recorded[k, s] = both[0] + both[1]

    row_at = lax.broadcasted_iota(jnp.int32, (rows, cols), 0)
    col_at = lax.broadcasted_iota(jnp.int32, (rows, cols), 1)

    def in_plane(x):
        around = jnp.where(row_at == rows - 1, 0.0, pltpu.roll(x, rows - 1, 0))
        around += jnp.where(row_at == 0, 0.0, pltpu.roll(x, 1, 0))
        around += jnp.where(col_at == cols - 1, 0.0, pltpu.roll(x, cols - 1, 1))
        around += jnp.where(col_at == 0, 0.0, pltpu.roll(x, 1, 1))
        return around

    def inner(earlier, current, s, z):
        x = current[s, z].astype(F32)
        around = in_plane(x)
        if z < last:
            around += current[s, z + 1].astype(F32)
        if z > 0:
            around += current[s, z - 1].astype(F32)
        return 2.0 * x - earlier[s, z].astype(F32) + courant[z] * (around - 6.0 * x)

    def near(halo, side, e, s):
        return halo[side, e, s, 1 - side]

    def begin(fields, j, s, source):
        for z in plane_range:
            partial[s, z] = inner(fields[j], fields[j + 1], s, z) + source(j, s, z + 1)

    def one_step(fields, link, j, s):
        halo, following = link[0], fields[j + 2]
        for z in plane_range:
            value = partial[s, z]
            if z == 0:
                value += courant[z] * halo[0, 0, s, j].astype(F32)
            if z == last:
                value += courant[z] * halo[1, 0, s, j].astype(F32)
            following[s, z] = value.astype(BF16)
        for side in sides:
            if j == 0:
                send(side, *plane_args(side, following, link, 1, s))
            else:
                send(side, *pair_args(side, following, link, 1, s))

    def two_steps(fields, link, rings, e, s, source, ring_source):
        halo = link[0]
        j = 2 * e
        earlier, current, middle, after = fields[j : j + 4]
        for z in plane_range:
            value = partial[s, z]
            if z == 0:
                value += courant[z] * near(halo, 0, e, s).astype(F32)
            if z == last:
                value += courant[z] * near(halo, 1, e, s).astype(F32)
            middle[s, z] = value.astype(BF16)
        for side in sides:
            x = near(halo, side, e, s).astype(F32)
            around = in_plane(x) + halo[side, e, s, side].astype(F32)
            around += current[s, 0 if side == 0 else last].astype(F32)
            old = halo[side, 0, s, 1] if e == 1 else rings[side, e - 1, s]
            value = 2.0 * x - old.astype(F32)
            value += courant_ring[side].astype(F32) * (around - 6.0 * x)
            rings[side, e, s] = (value + ring_source(e, s, side)).astype(BF16)
        for z in plane_range:
            value = inner(current, middle, s, z) + source(j + 1, s, z + 1)
            if z == 0:
                value += courant[z] * rings[0, e, s].astype(F32)
            if z == last:
                value += courant[z] * rings[1, e, s].astype(F32)
            after[s, z] = value.astype(BF16)
        if e < pairs - 1:
            for side in sides:
                send(side, *pair_args(side, after, link, e + 1, s))

    def fire(j, s, w):
        return signature[j] * fired[s, w]

    def fire_ring(e, s, side):
        return signature[2 * e] * fired[s, 0 if side == 0 else wide - 1]

    def correlate(k, s):
        top, bottom = 0.0, 0.0
        for z in plane_range:
            p = ahead[k + 2][s, z].astype(F32)
            top += p * recorded[k, s, z + 1]
            bottom += p * p * tally[z + 1]
        if k:
            top += products[s, 0]
            bottom += products[s, 1]
        products[s, 0] = top
        products[s, 1] = bottom

    for load in loads:
        load.wait()
    courant[...] = (velocity[...] * SPEED_SCALE) ** 2
    courant_edge[0] = courant[last].astype(BF16)
    courant_edge[1] = courant[0].astype(BF16)
    for s in shot_range:
        begin(ahead, 0, s, fire)

    for j in (0, 1):
        for s in shot_range:
            for side in sides:
                receive(side, *plane_args(side, ahead[j + 1], ahead_link, j, s))
            one_step(ahead, ahead_link, j, s)
            begin(ahead, j + 1, s, fire)
        if j == 0:
            for side in sides:
                send(side, *courant_args(side))
        record(2 * j)
        record(2 * j + 1)
    for s in shot_range:
        correlate(0, s)
        correlate(1, s)
    for side in sides:
        receive(side, *courant_args(side))

    for e in range(1, pairs):
        for s in shot_range:
            for side in sides:
                receive(side, *pair_args(side, ahead[2 * e + 1], ahead_link, e, s))
            two_steps(ahead, ahead_link, forward_ring, e, s, fire, fire_ring)
            if e < pairs - 1:
                begin(ahead, 2 * e + 2, s, fire)
        if e == 1:
            for s in shot_range:
                for side in sides:
                    send(side, *plane_args(side, terminal_in, back_link, 0, s))
            for k in range(4, ticks):
                record(k)
        for s in shot_range:
            correlate(2 * e, s)
            correlate(2 * e + 1, s)

    line = lax.broadcasted_iota(jnp.int32, (8, 128), 0)
    block = jnp.zeros((8, 128), F32)
    for s in shot_range:
        block = jnp.where(line == 2 * s, jnp.sum(products[s, 0]), block)
        block = jnp.where(line == 2 * s + 1, jnp.sum(products[s, 1]), block)
    sums[...] = block

    def share(d):
        return pltpu.make_async_remote_copy(
            src_ref=sums,
            dst_ref=gathered.at[me],
            send_sem=sums_sent.at[d],
            recv_sem=sums_got.at[me],
            device_id={"space": lax.rem(me + d, peers)},
            device_id_type=MESH,
        )

    def shared(d):
        other = lax.rem(me + d, peers)
        return pltpu.make_async_remote_copy(
            src_ref=sums,
            dst_ref=gathered.at[other],
            send_sem=sums_sent.at[d],
            recv_sem=sums_got.at[other],
            device_id={"space": other},
            device_id_type=MESH,
        )

    for d in range(1, peers):
        share(d).start()
    gathered[me] = block

    for s in shot_range:
        begin(back, 0, s, lambda j, s, w: -recorded[ticks - 1, s, w])
        for side in sides:
            receive(side, *plane_args(side, terminal_in, back_link, 0, s))

    for d in range(1, peers):
        shared(d).wait_recv()
    whole = gathered[0]
    for i in range(1, peers):
        whole += gathered[i]
    scales = []
    for s in shot_range:
        scale = whole[2 * s : 2 * s + 1] / (whole[2 * s + 1 : 2 * s + 2] + EPSILON)
        scales.append(scale[:, :1])
        amplitude[s] = jnp.max(scale)

    for s in shot_range:
        for z in plane_range:
            p = final[s, z].astype(F32)
            partial[s, z] = partial[s, z] + scales[s] * (tally[z + 1] * p)

    def residue(j, s, w):
        k = ticks - 1 - j
        p = ahead[k + 2][s, w - 1].astype(F32)
        return scales[s] * (tally[w] * p) - recorded[k, s, w]

    def residue_ring(e, s, side):
        w = 0 if side == 0 else wide - 1
        p = near(forward_halo, side, pairs - e, s)
        return scales[s] * (tally[w] * p.astype(F32)) - recorded[ticks - 1 - 2 * e, s, w]

    def gather_total(j, z):
        moment = ticks - 1 - j
        value = 0.0
        for s in shot_range:
            curvature = (
                ahead[moment + 2][s, z].astype(F32)
                - 2.0 * ahead[moment + 1][s, z].astype(F32)
                + ahead[moment][s, z].astype(F32)
            )
            value += back[j + 2][s, z].astype(F32) * curvature
        return value if j == 0 else total[z] + value

    def swap(z):
        return pltpu.make_async_remote_copy(
            src_ref=outgoing.at[z],
            dst_ref=incoming.at[z],
            send_sem=total_sent.at[z],
            recv_sem=total_got.at[z],
            device_id={"shot": 1 - core},
            device_id_type=MESH,
        )

    for j in (0, 1):
        for s in shot_range:
            if j:
                for side in sides:
                    receive(side, *plane_args(side, back[j + 1], back_link, j, s))
            one_step(back, back_link, j, s)
            begin(back, j + 1, s, residue)
        for z in plane_range:
            total[z] = gather_total(j, z)

    for e in range(1, pairs):
        for s in shot_range:
            for side in sides:
                receive(side, *pair_args(side, back[2 * e + 1], back_link, e, s))
            two_steps(back, back_link, backward_ring, e, s, residue, residue_ring)
            if e < pairs - 1:
                begin(back, 2 * e + 2, s, residue)
        for z in plane_range:
            total[z] = gather_total(2 * e, z)
            value = gather_total(2 * e + 1, z)
            if e < pairs - 1:
                total[z] = value
            else:
                outgoing[z] = value.astype(BF16)
                swap(z).start()

    for z in plane_range:
        weight = 2.0 * (1500.0 / velocity[z]) ** 3
        swap(z).wait_recv()
        gradient[z] = weight * (outgoing[z].astype(F32) + incoming[z].astype(F32))

    for side, args in started:

        @pl.when(me < peers - 1 if side == 0 else me > 0)
        def _(side=side, args=args):
            hop(side, *args).wait_send()

    for d in range(1, peers):
        share(d).wait_send()
    for z in plane_range:
        swap(z).wait_send()


def body(peers, *args):
    medium, entry, locations, recordings = args[0], args[2], args[7], args[8]
    shots, planes, rows, cols = entry.shape
    ticks = recordings.shape[1]
    probes = locations.shape[1]
    vmem = pl.BlockSpec(memory_space=pltpu.VMEM)
    smem = pl.BlockSpec(memory_space=pltpu.SMEM)
    slab = (planes, rows, cols)
    wide = (planes + 2, rows, cols)
    pairs = ticks // 2
    dma = pltpu.SemaphoreType.DMA
    return pl.pallas_call(
        functools.partial(kernel, peers),
        out_shape=(
            jax.ShapeDtypeStruct(entry.shape, BF16),
            jax.ShapeDtypeStruct((shots,), F32),
            jax.ShapeDtypeStruct(medium.shape, F32),
        ),
        in_specs=[pl.BlockSpec(memory_space=pl.ANY)] * 5 + [smem] + [vmem] * 3,
        out_specs=(vmem, smem, vmem),
        scratch_shapes=[
            pltpu.VMEM(slab, F32),
            pltpu.VMEM((shots,) + slab, BF16),
            pltpu.VMEM((shots,) + slab, BF16),
            pltpu.VMEM((shots,) + slab, BF16),
            pltpu.VMEM((shots,) + slab, BF16),
            pltpu.VMEM((ticks - 1, shots) + slab, BF16),
            pltpu.VMEM((ticks, shots) + slab, BF16),
            pltpu.VMEM((2, pairs, shots, 2, rows, cols), BF16),
            pltpu.VMEM((2, pairs, shots, 2, rows, cols), BF16),
            pltpu.VMEM((2, pairs, shots, rows, cols), BF16),
            pltpu.VMEM((2, pairs, shots, rows, cols), BF16),
            pltpu.VMEM((2, rows, cols), BF16),
            pltpu.VMEM(slab, F32),
            pltpu.VMEM((2, rows, cols), BF16),
            pltpu.VMEM((shots,) + slab, F32),
            pltpu.VMEM((cols, probes), BF16),
            pltpu.VMEM(wide, F32),
            pltpu.VMEM((shots,) + wide, F32),
            pltpu.VMEM((ticks, shots) + wide, F32),
            pltpu.VMEM((8, 128), F32),
            pltpu.VMEM((shots, 2, rows, cols), F32),
            pltpu.VMEM((peers, 8, 128), F32),
            pltpu.VMEM(slab, F32),
            pltpu.VMEM(slab, BF16),
            pltpu.VMEM(slab, BF16),
            dma((5,)),
            dma((2, pairs + 1, shots)),
            dma((2, pairs + 1, shots)),
            dma((2, pairs + 1, shots)),
            dma((2, pairs + 1, shots)),
            dma((2,)),
            dma((2,)),
            dma((peers,)),
            dma((peers,)),
            dma((planes,)),
            dma((planes,)),
        ],
        compiler_params=pltpu.CompilerParams(
            collective_id=0, has_side_effects=True, vmem_limit_bytes=40 * 1024 * 1024
        ),
    )(*args)


def solution(mesh):
    placed = (
        P("space", None, None),
        P("shot", "space", None, None),
        P("shot", "space", None, None),
        P("shot", "space", None, None),
        P("shot", "space", None, None),
        P(),
        P("shot", None),
        P(),
        P("shot", None, None),
    )
    return jax.shard_map(
        functools.partial(body, mesh.shape["space"]),
        mesh=mesh,
        in_specs=placed,
        out_specs=(P("shot", "space", None, None), P("shot"), P("space", None, None)),
        check_vma=False,
    )
```

```python
import functools

import jax
import jax.numpy as jnp
from jax import lax
from jax.experimental import pallas as pl
from jax.experimental.pallas import tpu as pltpu
from jax.sharding import PartitionSpec as P

SPEED_SCALE = 1.0 / 6000.0
EPSILON = 1e-06
MESH = pl.DeviceIdType.MESH
F32 = jnp.float32
BF16 = jnp.bfloat16


def kernel(
    peers,
    velocity_in,
    preceding_in,
    entry_in,
    beyond_in,
    terminal_in,
    signature,
    emitters,
    locations,
    recordings,
    final,
    amplitude,
    gradient,
    velocity,
    preceding,
    entry,
    beyond,
    terminal,
    forward,
    backward,
    forward_halo,
    backward_halo,
    forward_ring,
    backward_ring,
    courant_edge,
    courant,
    courant_ring,
    partial,
    column_hot,
    tally,
    fired,
    recorded,
    sums,
    products,
    gathered,
    total,
    outgoing,
    incoming,
    loaded,
    forward_sent,
    forward_got,
    backward_sent,
    backward_got,
    courant_sent,
    courant_got,
    sums_sent,
    sums_got,
    total_sent,
    total_got,
):
    me = lax.axis_index("space")
    core = lax.axis_index("shot")
    shots, planes, rows, cols = entry.shape
    ticks = recordings.shape[1]
    last = planes - 1
    shot_range, plane_range, sides = range(shots), range(planes), (0, 1)
    pairs = ticks // 2

    barrier = pltpu.get_barrier_semaphore()
    for d in range(1, peers):
        pl.semaphore_signal(
            barrier, inc=1, device_id={"space": lax.rem(me + d, peers)}, device_id_type=MESH
        )
    pl.semaphore_signal(barrier, inc=1, device_id={"shot": 1 - core}, device_id_type=MESH)

    loads = [
        pltpu.make_async_copy(source, target, loaded.at[i])
        for i, (source, target) in enumerate(
            (
                (velocity_in, velocity),
                (preceding_in, preceding),
                (entry_in, entry),
                (beyond_in, beyond),
                (terminal_in, terminal),
            )
        )
    ]
    for load in loads:
        load.start()

    pl.semaphore_wait(barrier, peers)

    def hop(side, source, target, sent, got):
        return pltpu.make_async_remote_copy(
            src_ref=source,
            dst_ref=target,
            send_sem=sent,
            recv_sem=got,
            device_id={"space": me + 1 if side == 0 else me - 1},
            device_id_type=MESH,
        )

    started = []

    def send(side, *args):
        @pl.when(me < peers - 1 if side == 0 else me > 0)
        def _():
            hop(side, *args).start()

        started.append((side, args))

    def receive(side, *args):
        @pl.when(me > 0 if side == 0 else me < peers - 1)
        def _():
            hop(side, *args).wait_recv()

    def pair_args(side, field, link, e, s):
        halo, sent, got = link
        low = planes - 2 if side == 0 else 0
        return (
            field.at[s, pl.ds(low, 2)],
            halo.at[side, e, s],
            sent.at[side, e, s],
            got.at[side, e, s],
        )

    def plane_args(side, field, link, j, s):
        halo, sent, got = link
        edge, at = last if side == 0 else 0, j * pairs
        return (
            field.at[s, edge],
            halo.at[side, 0, s, j],
            sent.at[side, at, s],
            got.at[side, at, s],
        )

    def courant_args(side):
        return (
            courant_edge.at[side],
            courant_ring.at[side],
            courant_sent.at[side],
            courant_got.at[side],
        )

    ahead = [preceding, entry] + [forward.at[j] for j in range(ticks - 1)] + [final]
    back = [beyond, terminal] + [backward.at[j] for j in range(ticks)]
    ahead_link = (forward_halo, forward_sent, forward_got)
    back_link = (backward_halo, backward_sent, backward_got)

    for s in shot_range:
        for side in sides:
            send(side, *plane_args(side, entry_in, ahead_link, 0, s))

    for side, here in ((0, me == 0), (1, me == peers - 1)):

        @pl.when(here)
        def _(side=side):
            for ring in (
                forward_halo,
                backward_halo,
                courant_ring,
            ):
                ring[side] = jnp.zeros_like(ring[side])

    probes = locations.shape[1]
    wide = planes + 2
    cells = wide * rows
    row_of = (locations[0:1, :] - me * planes + 1) * rows + locations[1:2, :]
    row_hot = lax.broadcasted_iota(jnp.int32, (cells, probes), 0) == row_of
    column_hot[...] = jnp.where(
        lax.broadcasted_iota(jnp.int32, (cols, probes), 0) == locations[2:3, :], 1.0, 0.0
    ).astype(BF16)

    def spread(left):
        return lax.dot_general(
            left, column_hot[...], (((1,), (1,)), ((), ())), preferred_element_type=F32
        )

    firing = emitters[...].astype(F32)
    lefts = [jnp.where(row_hot, 1.0, 0.0)]
    lefts += [jnp.where(row_hot, firing[s : s + 1], 0.0) for s in shot_range]
    placed = spread(jnp.concatenate(lefts, axis=0).astype(BF16))
    tally[...] = placed[:cells].reshape(wide, rows, cols)
    fired[...] = placed[cells:].reshape(shots, wide, rows, cols)

    def record(k):
        lefts = [
            jnp.where(row_hot, recordings[s, k : k + 1, :], 0.0).astype(BF16) for s in shot_range
        ]
        both = spread(jnp.concatenate(lefts, axis=0))
        recorded[k] = both.reshape(shots, wide, rows, cols)

    row_at = lax.broadcasted_iota(jnp.int32, (rows, cols), 0)
    col_at = lax.broadcasted_iota(jnp.int32, (rows, cols), 1)

    def in_plane(x):
        around = jnp.where(row_at == rows - 1, 0.0, pltpu.roll(x, rows - 1, 0))
        around += jnp.where(row_at == 0, 0.0, pltpu.roll(x, 1, 0))
        around += jnp.where(col_at == cols - 1, 0.0, pltpu.roll(x, cols - 1, 1))
        around += jnp.where(col_at == 0, 0.0, pltpu.roll(x, 1, 1))
        return around

    def inner(earlier, current, s, z):
        x = current[s, z].astype(F32)
        around = in_plane(x)
        if z < last:
            around += current[s, z + 1].astype(F32)
        if z > 0:
            around += current[s, z - 1].astype(F32)
        return 2.0 * x - earlier[s, z].astype(F32) + courant[z] * (around - 6.0 * x)

    def near(halo, side, e, s):
        return halo[side, e, s, 1 - side]

    def begin(fields, j, s, source):
        for z in plane_range:
            partial[s, z] = inner(fields[j], fields[j + 1], s, z) + source(j, s, z + 1)

    def one_step(fields, link, j, s):
        halo, following = link[0], fields[j + 2]
        for z in plane_range:
            value = partial[s, z]
            if z == 0:
                value += courant[z] * halo[0, 0, s, j].astype(F32)
            if z == last:
                value += courant[z] * halo[1, 0, s, j].astype(F32)
            following[s, z] = value.astype(BF16)
        for side in sides:
            if j == 0:
                send(side, *plane_args(side, following, link, 1, s))
            else:
                send(side, *pair_args(side, following, link, 1, s))

    def two_steps(fields, link, rings, e, s, source, ring_source):
        halo = link[0]
        j = 2 * e
        earlier, current, middle, after = fields[j : j + 4]
        for z in plane_range:
            value = partial[s, z]
            if z == 0:
                value += courant[z] * near(halo, 0, e, s).astype(F32)
            if z == last:
                value += courant[z] * near(halo, 1, e, s).astype(F32)
            middle[s, z] = value.astype(BF16)
        for side in sides:
            x = near(halo, side, e, s).astype(F32)
            around = in_plane(x) + halo[side, e, s, side].astype(F32)
            around += current[s, 0 if side == 0 else last].astype(F32)
            old = halo[side, 0, s, 1] if e == 1 else rings[side, e - 1, s]
            value = 2.0 * x - old.astype(F32)
            value += courant_ring[side].astype(F32) * (around - 6.0 * x)
            rings[side, e, s] = (value + ring_source(e, s, side)).astype(BF16)
        for z in plane_range:
            value = inner(current, middle, s, z) + source(j + 1, s, z + 1)
            if z == 0:
                value += courant[z] * rings[0, e, s].astype(F32)
            if z == last:
                value += courant[z] * rings[1, e, s].astype(F32)
            after[s, z] = value.astype(BF16)
        if e < pairs - 1:
            for side in sides:
                send(side, *pair_args(side, after, link, e + 1, s))

    def fire(j, s, w):
        return signature[j] * fired[s, w]

    def fire_ring(e, s, side):
        return signature[2 * e] * fired[s, 0 if side == 0 else wide - 1]

    def correlate(k, s):
        top, bottom = 0.0, 0.0
        for z in plane_range:
            p = ahead[k + 2][s, z].astype(F32)
            top += p * recorded[k, s, z + 1]
            bottom += p * p * tally[z + 1]
        if k:
            top += products[s, 0]
            bottom += products[s, 1]
        products[s, 0] = top
        products[s, 1] = bottom

    for load in loads:
        load.wait()
    courant[...] = (velocity[...] * SPEED_SCALE) ** 2
    courant_edge[0] = courant[last].astype(BF16)
    courant_edge[1] = courant[0].astype(BF16)
    for s in shot_range:
        begin(ahead, 0, s, fire)

    for j in (0, 1):
        for s in shot_range:
            for side in sides:
                receive(side, *plane_args(side, ahead[j + 1], ahead_link, j, s))
            one_step(ahead, ahead_link, j, s)
            begin(ahead, j + 1, s, fire)
        if j == 0:
            for side in sides:
                send(side, *courant_args(side))
        record(2 * j)
        record(2 * j + 1)
    for s in shot_range:
        correlate(0, s)
        correlate(1, s)
    for side in sides:
        receive(side, *courant_args(side))

    for e in range(1, pairs):
        for s in shot_range:
            for side in sides:
                receive(side, *pair_args(side, ahead[2 * e + 1], ahead_link, e, s))
            two_steps(ahead, ahead_link, forward_ring, e, s, fire, fire_ring)
            if e < pairs - 1:
                begin(ahead, 2 * e + 2, s, fire)
        if e == 1:
            for s in shot_range:
                for side in sides:
                    send(side, *plane_args(side, terminal_in, back_link, 0, s))
            for k in range(4, ticks):
                record(k)
        for s in shot_range:
            correlate(2 * e, s)
            correlate(2 * e + 1, s)

    line = lax.broadcasted_iota(jnp.int32, (8, 128), 0)
    block = jnp.zeros((8, 128), F32)
    for s in shot_range:
        block = jnp.where(line == 2 * s, jnp.sum(products[s, 0]), block)
        block = jnp.where(line == 2 * s + 1, jnp.sum(products[s, 1]), block)
    sums[...] = block

    def share(d):
        return pltpu.make_async_remote_copy(
            src_ref=sums,
            dst_ref=gathered.at[me],
            send_sem=sums_sent.at[d],
            recv_sem=sums_got.at[me],
            device_id={"space": lax.rem(me + d, peers)},
            device_id_type=MESH,
        )

    def shared(d):
        other = lax.rem(me + d, peers)
        return pltpu.make_async_remote_copy(
            src_ref=sums,
            dst_ref=gathered.at[other],
            send_sem=sums_sent.at[d],
            recv_sem=sums_got.at[other],
            device_id={"space": other},
            device_id_type=MESH,
        )

    for d in range(1, peers):
        share(d).start()
    gathered[me] = block

    for s in shot_range:
        begin(back, 0, s, lambda j, s, w: -recorded[ticks - 1, s, w])
        for side in sides:
            receive(side, *plane_args(side, terminal_in, back_link, 0, s))

    for d in range(1, peers):
        shared(d).wait_recv()
    whole = gathered[0]
    for i in range(1, peers):
        whole += gathered[i]
    scales = []
    for s in shot_range:
        scale = whole[2 * s : 2 * s + 1] / (whole[2 * s + 1 : 2 * s + 2] + EPSILON)
        scales.append(scale[:, :1])
        amplitude[s] = jnp.max(scale)

    for s in shot_range:
        for z in plane_range:
            p = final[s, z].astype(F32)
            partial[s, z] = partial[s, z] + scales[s] * (tally[z + 1] * p)

    def residue(j, s, w):
        k = ticks - 1 - j
        p = ahead[k + 2][s, w - 1].astype(F32)
        return scales[s] * (tally[w] * p) - recorded[k, s, w]

    def residue_ring(e, s, side):
        w = 0 if side == 0 else wide - 1
        p = near(forward_halo, side, pairs - e, s)
        return scales[s] * (tally[w] * p.astype(F32)) - recorded[ticks - 1 - 2 * e, s, w]

    def gather_total(j, z):
        moment = ticks - 1 - j
        value = 0.0
        for s in shot_range:
            curvature = (
                ahead[moment + 2][s, z].astype(F32)
                - 2.0 * ahead[moment + 1][s, z].astype(F32)
                + ahead[moment][s, z].astype(F32)
            )
            value += back[j + 2][s, z].astype(F32) * curvature
        return value if j == 0 else total[z] + value

    def swap(z):
        return pltpu.make_async_remote_copy(
            src_ref=outgoing.at[z],
            dst_ref=incoming.at[z],
            send_sem=total_sent.at[z],
            recv_sem=total_got.at[z],
            device_id={"shot": 1 - core},
            device_id_type=MESH,
        )

    for j in (0, 1):
        for s in shot_range:
            if j:
                for side in sides:
                    receive(side, *plane_args(side, back[j + 1], back_link, j, s))
            one_step(back, back_link, j, s)
            begin(back, j + 1, s, residue)
        for z in plane_range:
            total[z] = gather_total(j, z)

    for e in range(1, pairs):
        for s in shot_range:
            for side in sides:
                receive(side, *pair_args(side, back[2 * e + 1], back_link, e, s))
            two_steps(back, back_link, backward_ring, e, s, residue, residue_ring)
            if e < pairs - 1:
                begin(back, 2 * e + 2, s, residue)
        for z in plane_range:
            total[z] = gather_total(2 * e, z)
            value = gather_total(2 * e + 1, z)
            if e < pairs - 1:
                total[z] = value
            else:
                outgoing[z] = value.astype(BF16)
                swap(z).start()

    for z in plane_range:
        weight = 2.0 * (1500.0 / velocity[z]) ** 3
        swap(z).wait_recv()
        gradient[z] = weight * (outgoing[z].astype(F32) + incoming[z].astype(F32))

    for side, args in started:

        @pl.when(me < peers - 1 if side == 0 else me > 0)
        def _(side=side, args=args):
            hop(side, *args).wait_send()

    for d in range(1, peers):
        share(d).wait_send()
    for z in plane_range:
        swap(z).wait_send()


def body(peers, *args):
    medium, entry, locations, recordings = args[0], args[2], args[7], args[8]
    shots, planes, rows, cols = entry.shape
    ticks = recordings.shape[1]
    probes = locations.shape[1]
    vmem = pl.BlockSpec(memory_space=pltpu.VMEM)
    smem = pl.BlockSpec(memory_space=pltpu.SMEM)
    slab = (planes, rows, cols)
    wide = (planes + 2, rows, cols)
    pairs = ticks // 2
    dma = pltpu.SemaphoreType.DMA
    return pl.pallas_call(
        functools.partial(kernel, peers),
        out_shape=(
            jax.ShapeDtypeStruct(entry.shape, BF16),
            jax.ShapeDtypeStruct((shots,), F32),
            jax.ShapeDtypeStruct(medium.shape, F32),
        ),
        in_specs=[pl.BlockSpec(memory_space=pl.ANY)] * 5 + [smem] + [vmem] * 3,
        out_specs=(vmem, smem, vmem),
        scratch_shapes=[
            pltpu.VMEM(slab, F32),
            pltpu.VMEM((shots,) + slab, BF16),
            pltpu.VMEM((shots,) + slab, BF16),
            pltpu.VMEM((shots,) + slab, BF16),
            pltpu.VMEM((shots,) + slab, BF16),
            pltpu.VMEM((ticks - 1, shots) + slab, BF16),
            pltpu.VMEM((ticks, shots) + slab, BF16),
            pltpu.VMEM((2, pairs, shots, 2, rows, cols), BF16),
            pltpu.VMEM((2, pairs, shots, 2, rows, cols), BF16),
            pltpu.VMEM((2, pairs, shots, rows, cols), BF16),
            pltpu.VMEM((2, pairs, shots, rows, cols), BF16),
            pltpu.VMEM((2, rows, cols), BF16),
            pltpu.VMEM(slab, F32),
            pltpu.VMEM((2, rows, cols), BF16),
            pltpu.VMEM((shots,) + slab, F32),
            pltpu.VMEM((cols, probes), BF16),
            pltpu.VMEM(wide, F32),
            pltpu.VMEM((shots,) + wide, F32),
            pltpu.VMEM((ticks, shots) + wide, F32),
            pltpu.VMEM((8, 128), F32),
            pltpu.VMEM((shots, 2, rows, cols), F32),
            pltpu.VMEM((peers, 8, 128), F32),
            pltpu.VMEM(slab, F32),
            pltpu.VMEM(slab, BF16),
            pltpu.VMEM(slab, BF16),
            dma((5,)),
            dma((2, pairs + 1, shots)),
            dma((2, pairs + 1, shots)),
            dma((2, pairs + 1, shots)),
            dma((2, pairs + 1, shots)),
            dma((2,)),
            dma((2,)),
            dma((peers,)),
            dma((peers,)),
            dma((planes,)),
            dma((planes,)),
        ],
        compiler_params=pltpu.CompilerParams(
            collective_id=0, has_side_effects=True, vmem_limit_bytes=40 * 1024 * 1024
        ),
    )(*args)


def solution(mesh):
    placed = (
        P("space", None, None),
        P("shot", "space", None, None),
        P("shot", "space", None, None),
        P("shot", "space", None, None),
        P("shot", "space", None, None),
        P(),
        P("shot", None),
        P(),
        P("shot", None, None),
    )
    return jax.shard_map(
        functools.partial(body, mesh.shape["space"]),
        mesh=mesh,
        in_specs=placed,
        out_specs=(P("shot", "space", None, None), P("shot"), P("space", None, None)),
        check_vma=False,
    )
```
